32 devices in a mesh: groups: 2 (over y), cells: 4 (over z), sub: 2 (over x), lev: 2 (over core).
Axes of the slice: x: 2, y: 2, z: 4, core: 2. Of those that a mesh axis runs over, the one named last changes fastest.
Arguments:
- tracers: float32 [2, 80, 8192], P(None, 'lev', ('groups', 'cells', 'sub')), parts along dimension 2, may hold values from -6 to 6
- thickness: float32 [80, 8192], P('lev', ('groups', 'cells', 'sub')), parts along dimension 1, may hold values from 0.5 to 1.5
- ssh: float32 [8192], P(('groups', 'cells', 'sub')), parts along dimension 0, may hold values from -3 to 3
- potential: float32 [8192], P(('groups', 'cells', 'sub')), parts along dimension 0, may hold values from -6 to 6
- neighbours: int32 [6, 4096], P(None, ('cells', 'sub')), may hold values from 0 to 640, as said below
- edge_weight: float32 [6, 4096], P(None, ('cells', 'sub')), may hold values from 0.5 to 2
- send_list: int32 [2, 512], P(None, ('cells', 'sub')), may hold values from 0 to 511
- remap_src: int32 [8192], P(('cells', 'sub')), may hold values from 0 to 511
- remap_owner: int32 [8192, 1], P(('cells', 'sub')), may hold values from 0 to 7; in each aligned block of 1024 rows (0 to 1023, 1024 to 2047, ...) at most 384 rows name the same one
- remap_local: int32 [8192], P(('cells', 'sub')), may hold values from 0 to 511
- remap_weight: float32 [8192], P(('cells', 'sub')), may hold values from 0.2 to 1
Outputs:
- tracers_new: float32 [2, 80, 8192], P(None, 'lev', ('groups', 'cells', 'sub')), parts along dimension 2
- thickness_new: float32 [80, 8192], P('lev', ('groups', 'cells', 'sub')), parts along dimension 1
- ssh_new: float32 [8192], P(('groups', 'cells', 'sub')), parts along dimension 0
- atm_flux: float32 [4, 8192], P(None, ('groups', 'cells', 'sub')), parts along dimension 1
The draws below stay inside these ranges and needn't reach their ends.
There are 2 independent parts, one for each index of `groups`. The reference program is written for one: setup_inputs(seed, part) draws one part's arguments, and reference() takes and returns one part's arrays. A program takes and returns all parts, laid end to end along the dimension named above; an argument that names none is the same for every part. Nothing has to cross between parts.
Inputs may be any that keep to these rules, and one draw needn't show every extreme that they name: `neighbours`: A value below 512 is an owned cell, 512 + k the k-th cell of the previous partition's row 1 list, 576 + k the k-th cell of the next partition's row 0 list, and 640 an empty edge slot. `remap_owner`: the entries of one partition name each owner at most 384 times, and in every draw some partition names some owner exactly 384 times.
All inputs are finite; a program needn't handle non-finite values.
Results may differ from the reference program's by a relative error of at most 0.0003.
Values sent between devices are 32-bit elements; how exact they have to be, the bound alone decides.
A program may use at most 128 MiB of HBM per device.

```python
import math
import jax
import jax.numpy as jnp
import numpy as np
from jax import lax

CELL_DEV = 512
HALO = 64
LEV = 80
EDGES = 6
SUBCYCLES = 10
FLUXES = 4
REMAP_DEV = 1024
ATM_DEV = 512
PARTITIONS = 8
OCEAN_CELLS = 4096
ATM_CELLS = 4096
ENTRIES = 8192
CAPACITY = 384


def draw_neighbours(key, part):
    key = jax.random.fold_in(key, 7)
    first_key, second_key, third_key = jax.random.split(key, 3)
    table_shape = (EDGES, OCEAN_CELLS)
    kind_draw = jax.random.randint(first_key, table_shape, 0, 100)
    owned = jax.random.randint(second_key, table_shape, 0, CELL_DEV)
    rimmed = jax.random.randint(third_key, table_shape, CELL_DEV, CELL_DEV + 2 * HALO)
    return jnp.where(kind_draw < 70, owned, jnp.where(kind_draw < 92, rimmed, CELL_DEV + 2 * HALO)).astype(jnp.int32)


def set_ends(entries, own_key, smallest, high):
    index_at = [jax.random.randint(jax.random.fold_in(own_key, axis), (), 0, length) for axis, length in enumerate(entries.shape)]
    widest = entries.shape.index(max(entries.shape))
    beside = index_at[:widest] + [(index_at[widest] + 1) % entries.shape[widest]] + index_at[widest + 1:]
    return entries.at[tuple(index_at)].set(smallest).at[tuple(beside)].set(high)


def level_of(key, dims, pieces, smallest, high):
    def one(dim, parts):
        heights = jax.random.uniform(jax.random.fold_in(jax.random.fold_in(key, 6), dim), (parts,), jnp.float32, smallest / len(pieces), high / len(pieces))
        return jnp.repeat(jnp.exp(heights), dims[dim] // parts).reshape((-1,) + (1,) * (len(dims) - dim - 1))

    gain = one(*pieces[0])
    for cut in pieces[1:]:
        gain = gain * one(*cut)
    return gain


def shared_out(own_key, own, number, rows, count, top, most, lean):
    order = jax.random.permutation(own_key, count)
    crowded, usual = load_shares(count, rows * top, most, lean, True), load_shares(count, rows * top, most, lean, False)
    places = jnp.arange(count)

    def named(tallies, offset_by):
        used = int((tallies > 0).sum())
        fixed = max(1, used // 4)
        moved = fixed + (places - fixed + offset_by * (used - fixed)) % max(1, count - fixed)
        return jnp.zeros((count,), jnp.int32).at[order[jnp.where(places < fixed, places, moved)]].set(jnp.asarray(tallies, jnp.int32))

    tallies = jnp.where(number % 4 == 0, named(crowded, number // 4), named(usual, number - number // 4 - 1))
    mixed = jax.random.permutation(jax.random.fold_in(own, 3), count)
    source_of, taker = mixed[0:count // 2 * 2:2], mixed[1:count // 2 * 2:2]
    slack = jnp.minimum(tallies[source_of] - 1, most - tallies[taker]) // 2
    slack = jnp.where((source_of == order[0]) | (taker == order[0]) | (tallies[taker] == 0), 0, jnp.maximum(slack, 0))
    moved = jax.random.randint(jax.random.fold_in(own, 4), (count // 2,), 0, 1 << 20) % (slack + 1)
    tallies = tallies.at[source_of].add(-moved).at[taker].add(moved)
    labels = jnp.searchsorted(jnp.cumsum(tallies), jnp.arange(rows * top), side="right").astype(jnp.int32)
    listing = labels.reshape(top, rows).T
    listing = listing[jax.random.permutation(jax.random.fold_in(own, 1), rows)]
    offset_by = jax.random.randint(jax.random.fold_in(own, 2), (rows, 1), 0, top)
    return jnp.take_along_axis(listing, (jnp.arange(top)[None, :] + offset_by) % top, axis=1)


def load_shares(number_of, total, reach, slope, full):
    weights = [(1 << 20) // math.isqrt(rank ** slope) + 1 for rank in range(1, number_of + 1)]
    largest = reach if full else min(reach, max(-(-total // number_of), total * weights[0] // sum(weights)))
    least = 1 if total - largest >= number_of - 1 else 0
    given, rest = [largest] + [least] * (number_of - 1), total - largest - least * (number_of - 1)
    while rest > 0:
        movable = [i for i in range(1, number_of) if given[i] < largest] or [i for i in range(1, number_of) if given[i] < reach]
        mass, left = sum([weights[i] for i in movable]), rest
        for i in movable:
            extra = min(reach - given[i], max(1, left * weights[i] // mass), rest)
            given[i] = given[i] + extra
            rest = rest - extra
    return np.array(given)


def scatter_about(stream_key, dims, deviation, bound, cuts=(), kind=jnp.bfloat16):
    loudness = level_of(stream_key, dims, cuts, -0.22, 0.18) if cuts else 1.0
    array = jax.random.normal(stream_key, dims, jnp.float32) * deviation * loudness
    return jnp.minimum(jnp.maximum(array, -bound), bound).astype(kind)


def setup_inputs(seed: int = 0, part: int = 0) -> dict:
    key_of = jax.random.split(jax.random.key(seed), 12)
    part_keys = jax.random.split(jax.random.fold_in(key_of[11], part), 12)
    tracers = scatter_about(part_keys[0], (2, LEV, OCEAN_CELLS), 1.0, 6.0, ((1, 2), (2, 8)), jnp.float32)
    thickness = jnp.clip(0.5 + 1.0 * jax.random.uniform(part_keys[1], (LEV, OCEAN_CELLS), jnp.float32) ** level_of(part_keys[1], (LEV, OCEAN_CELLS), ((0, 2), (1, 8)), -0.2, 0.2), 0.5, 1.5)
    ssh = scatter_about(part_keys[2], (OCEAN_CELLS,), 0.5, 3.0, ((0, 8),), jnp.float32)
    potential = scatter_about(part_keys[3], (OCEAN_CELLS,), 1.0, 6.0, ((0, 8),), jnp.float32)
    neighbours = draw_neighbours(jax.random.fold_in(key_of[11], 71), part)
    edge_weight = jnp.clip(jnp.exp(math.log(2.0) - 1.3862944 * jax.random.uniform(key_of[5], (EDGES, OCEAN_CELLS), jnp.float32) ** level_of(key_of[5], (EDGES, OCEAN_CELLS), ((1, 8),), -0.2, 0.2)), 0.5, 2.0)
    send_list = set_ends(jax.random.randint(key_of[6], (2, PARTITIONS * HALO), 0, CELL_DEV), jax.random.fold_in(key_of[6], 1), 0, CELL_DEV - 1).astype(jnp.int32)
    remap_src = set_ends(jax.random.randint(key_of[7], (ENTRIES,), 0, CELL_DEV), jax.random.fold_in(key_of[7], 1), 0, CELL_DEV - 1).astype(jnp.int32)
    remap_owner_keys = jax.random.split(jax.random.fold_in(key_of[8], 1), ENTRIES // REMAP_DEV)
    remap_owner_turns = jax.random.permutation(jax.random.fold_in(key_of[8], 3), ENTRIES // REMAP_DEV)
    remap_owner = jax.vmap(lambda own, number: shared_out(jax.random.fold_in(key_of[8], 2), own, number, REMAP_DEV, PARTITIONS, 1, CAPACITY, 2))(remap_owner_keys, remap_owner_turns).reshape((ENTRIES, 1))
    remap_local = set_ends(jax.random.randint(key_of[9], (ENTRIES,), 0, ATM_DEV), jax.random.fold_in(key_of[9], 1), 0, ATM_DEV - 1).astype(jnp.int32)
    remap_weight = jnp.clip(0.2 + 0.8 * jax.random.uniform(key_of[10], (ENTRIES,), jnp.float32) ** level_of(key_of[10], (ENTRIES,), ((0, 8),), -0.2, 0.2), 0.2, 1.0)
    return dict(tracers=tracers, thickness=thickness, ssh=ssh, potential=potential, neighbours=neighbours, edge_weight=edge_weight, send_list=send_list, remap_src=remap_src, remap_owner=remap_owner, remap_local=remap_local, remap_weight=remap_weight)


thermal = 0.2
haline = 0.15
time_step = 0.05
mixing = 0.5
fast_step = 0.15


def extend(blocks, sends):
    members = jnp.arange(blocks.shape[1], dtype=jnp.int32)[:, None]
    to_left = blocks[:, members, sends[0]]
    to_right = blocks[:, members, sends[1]]
    blank = jnp.zeros_like(to_left[:, :1])
    from_left = jnp.concatenate([blank, to_right[:, :-1]], axis=1)
    from_right = jnp.concatenate([to_left[:, 1:], blank], axis=1)
    padding = jnp.zeros(blocks.shape[:2] + (1,), blocks.dtype)
    return jnp.concatenate([blocks, from_left, from_right, padding], axis=2)


def stencil(extended, neighbours, edge_weight):
    levels = extended.shape[0] // 4
    cell_count = neighbours.shape[1]
    blank_slot = extended.shape[1] - 1
    tracer_own = extended[:2 * levels, :cell_count]
    height_own = extended[2 * levels:3 * levels, :cell_count]
    mont_own = extended[3 * levels:, :cell_count]
    advect = jnp.zeros_like(tracer_own)
    laplace = jnp.zeros_like(tracer_own)
    height_rate = jnp.zeros_like(height_own)
    for edge_slot in range(neighbours.shape[0]):
        near_index = neighbours[edge_slot]
        coupling = edge_weight[edge_slot] * (near_index < blank_slot).astype(jnp.float32)
        gathered = extended[:, near_index]
        tracer_near = gathered[:2 * levels]
        height_near = gathered[2 * levels:3 * levels]
        mont_near = gathered[3 * levels:]
        normal_flow = -coupling[None, :] * (mont_near - mont_own)
        height_rate = height_rate - normal_flow * (0.5 * (height_near + height_own))
        both_flow = jnp.concatenate([normal_flow, normal_flow], axis=0)
        advect = advect - 0.5 * both_flow * (tracer_near - tracer_own)
        laplace = laplace + coupling[None, :] * (tracer_near - tracer_own)
    return advect, laplace, height_rate


def local_block(item):
    return stencil(item[0], item[1], item[2])


def reference(tracers, thickness, ssh, potential, neighbours, edge_weight, send_list, remap_src, remap_owner, remap_local, remap_weight):
    buoyancy = thermal * tracers[0] - haline * tracers[1]
    layer_load = buoyancy * thickness
    pressure = jnp.cumsum(layer_load, axis=0) - 0.5 * layer_load
    montgomery = pressure + ssh[None, :]
    old_tracers = tracers.reshape(2 * LEV, OCEAN_CELLS)
    stacked = jnp.concatenate([old_tracers, thickness, montgomery], axis=0)
    sends = send_list.reshape(2, PARTITIONS, HALO)
    extended = extend(stacked.reshape(4 * LEV, PARTITIONS, CELL_DEV), sends)
    near_table = neighbours.reshape(EDGES, PARTITIONS, CELL_DEV)
    weights = edge_weight.reshape(EDGES, PARTITIONS, CELL_DEV)
    advect, laplace, height_rate = lax.map(local_block, (jnp.moveaxis(extended, 1, 0), jnp.moveaxis(near_table, 1, 0), jnp.moveaxis(weights, 1, 0)))
    advect = jnp.moveaxis(advect, 0, 1).reshape(2 * LEV, OCEAN_CELLS)
    laplace = jnp.moveaxis(laplace, 0, 1).reshape(2 * LEV, OCEAN_CELLS)
    height_rate = jnp.moveaxis(height_rate, 0, 1).reshape(LEV, OCEAN_CELLS)
    new_tracers = old_tracers + time_step * (advect + mixing * laplace)
    provisional = thickness + time_step * height_rate
    forcing = jnp.sum(thickness * montgomery, axis=0) / LEV
    column = jnp.sum(provisional, axis=0)
    heat_sum = jnp.sum(provisional * new_tracers[:LEV], axis=0)
    salt_sum = jnp.sum(provisional * new_tracers[LEV:], axis=0)
    heat_plain = jnp.sum(new_tracers[:LEV], axis=0)
    salt_plain = jnp.sum(new_tracers[LEV:], axis=0)
    coupling_all = weights * (near_table < CELL_DEV + 2 * HALO).astype(jnp.float32)
    potential_now = potential.reshape(PARTITIONS, CELL_DEV)
    height_now = ssh.reshape(PARTITIONS, CELL_DEV)
    forcing_grid = forcing.reshape(PARTITIONS, CELL_DEV)
    for step_index in range(SUBCYCLES):
        potential_now = potential_now - fast_step * (height_now + forcing_grid)
        padded = extend(potential_now[None], sends)[0]
        divergence = jnp.zeros_like(potential_now)
        for edge_slot in range(EDGES):
            near_values = jnp.take_along_axis(padded, near_table[edge_slot], axis=1)
            divergence = divergence + coupling_all[edge_slot] * (near_values - potential_now)
        height_now = height_now + fast_step * divergence
    ssh_new = height_now.reshape(OCEAN_CELLS)
    potential_new = potential_now.reshape(OCEAN_CELLS)
    correction = (LEV + ssh_new - column) / LEV
    thickness_new = provisional + correction[None, :]
    surface = jnp.stack([ssh_new, potential_new, (heat_sum + correction * heat_plain) / LEV, (salt_sum + correction * salt_plain) / LEV])
    entry_part = jnp.arange(ENTRIES, dtype=jnp.int32) // REMAP_DEV
    contrib = remap_weight[None, :] * surface[:, entry_part * CELL_DEV + remap_src]
    target = remap_owner[:, 0] * ATM_DEV + remap_local
    atm_flux = jnp.zeros((FLUXES, ATM_CELLS), jnp.float32).at[:, target].add(contrib)
    return new_tracers.reshape(2, LEV, OCEAN_CELLS), thickness_new, ssh_new, atm_flux
```

```python
import functools

import jax
import jax.numpy as jnp
from jax import lax
from jax.experimental import pallas as pl
from jax.experimental.pallas import tpu as pltpu
from jax.sharding import PartitionSpec as P

SUBCYCLES = 10

thermal = 0.2
haline = 0.15
time_step = 0.05
mixing = 0.5
fast_step = 0.15

F32 = jnp.float32
BF16 = jnp.bfloat16
LANES = 128


def repeat(count, body):
    if count <= 16:
        for i in range(count):
            body(i)
    else:

        def step(i, carry):
            body(i)
            return carry

        lax.fori_loop(0, count, step, 0)


def guarded(flag, body):
    if flag is True:
        body()
    else:
        pl.when(flag)(body)


def split(x):
    high = x.astype(BF16)
    return high, (x - high.astype(F32)).astype(BF16)


def lanes_of(x, index):
    return jnp.take_along_axis(x, index, axis=1, mode="promise_in_bounds")


def ocean_kernel(
    n_cells,
    n_sub,
    reach,
    window,
    tr_ref,
    th_ref,
    ssh_ref,
    pot_ref,
    near_ref,
    ew_ref,
    send_ref,
    src_ref,
    own_ref,
    loc_ref,
    rw_ref,
    tr_out,
    th_out,
    ssh_out,
    atm_out,
    halo_send,
    halo_recv,
    table_all,
    state_mine,
    state_all,
    col_mine,
    col_other,
    flux_send,
    flux_recv,
    x_all,
    x_split,
    hot,
    prov_ref,
    flux_lhs,
    flux_hot,
    halo_ss,
    halo_rs,
    table_ss,
    table_rs,
    state_ss,
    state_rs,
    col_ss,
    col_rs,
    flux_ss,
    flux_rs,
):
    members = n_cells * n_sub
    levels, cells = th_ref.shape
    edges = near_ref.shape[0]
    chunks = cells // LANES
    halo = send_ref.shape[1] // 2
    full_levels = 2 * levels
    q = lax.axis_index("cells") * n_sub + lax.axis_index("sub")
    lev = lax.axis_index("lev")
    whole = window == members

    def at(p, level):
        return {"cells": lax.div(p, n_sub), "sub": lax.rem(p, n_sub), "lev": level}

    def slot_of(source, target):
        return source if whole else source - target + reach

    mine = slot_of(q, q)

    def window_partner(i):
        if whole:
            return lax.rem(q + i, members), True
        d = i - reach
        p = q + d
        ok = (p >= 0) & (p < members)
        return jnp.clip(p, 0, members - 1), ok

    same = range(1, members) if whole else [i for i in range(window) if i != reach]
    both = range(window)

    barrier = pltpu.get_barrier_semaphore()

    def greet(i):
        p = lax.rem(q + 1 + i, members)
        pl.semaphore_signal(
            barrier, inc=1, device_id=at(p, lev), device_id_type=pl.DeviceIdType.MESH
        )

    repeat(members - 1, greet)
    for i in both:
        p, ok = window_partner(i)
        guarded(
            ok,
            lambda p=p: pl.semaphore_signal(
                barrier, inc=1, device_id=at(p, 1 - lev), device_id_type=pl.DeviceIdType.MESH
            ),
        )
    if whole:
        greetings = members - 1 + window
    else:
        greetings = (
            members
            - 1
            + jnp.minimum(q + reach, members - 1)
            - jnp.maximum(q - reach, 0)
            + 1
        )

    row8 = lax.broadcasted_iota(jnp.int32, (8, LANES), 0)
    lane8 = lax.broadcasted_iota(jnp.int32, (8, LANES), 1)
    upper = row8 < 4
    chunk8 = jnp.where(upper, row8, row8 - 4)
    left8 = lane8 < halo

    def pair(v):
        r = pltpu.roll(v, 4, 0)
        return jnp.where(upper, v, r), jnp.where(upper, r, v)

    def put_rows(ref, start, row):
        for c in range(chunks):
            ref[start + c : start + c + 1, :] = row[:, c * LANES : (c + 1) * LANES]

    temp = tr_ref[0]
    salt = tr_ref[1]
    thick = th_ref[...]
    load = (thermal * temp - haline * salt) * thick
    rows = lax.broadcasted_iota(jnp.int32, (levels, levels), 0)
    cols = lax.broadcasted_iota(jnp.int32, (levels, levels), 1)
    below = jnp.where(cols < rows, 1.0, jnp.where(cols == rows, 0.5, 0.0)).astype(F32)
    pressure = lax.dot_general(
        below,
        load,
        (((1,), (0,)), ((), ())),
        precision=lax.Precision.HIGHEST,
        preferred_element_type=F32,
    )
    ssh_row = jnp.concatenate([ssh_ref[c : c + 1, :] for c in range(chunks)], axis=1)
    part_mont = pressure + ssh_row
    x_all[0:levels, 0:cells] = temp
    x_all[levels : 2 * levels, 0:cells] = salt
    x_all[2 * levels : 3 * levels, 0:cells] = thick
    x_all[3 * levels : 4 * levels, 0:cells] = part_mont

    state_mine[0:4, :] = ssh_ref[...]
    state_mine[4:8, :] = pot_ref[...]
    put_rows(state_mine, 8, jnp.sum(thick * part_mont, axis=0, keepdims=True))
    put_rows(state_mine, 12, jnp.sum(load, axis=0, keepdims=True))
    put_rows(state_mine, 16, jnp.sum(thick, axis=0, keepdims=True))
    state_mine[20:24, :] = jnp.zeros((4, LANES), F32)

    my_table = table_all.at[mine]
    blank_slot = cells + 2 * halo
    for e in range(edges):
        index_row = near_ref[e : e + 1, :]
        weight = jnp.where(index_row < blank_slot, ew_ref[e : e + 1, :], 0.0)
        put_rows(my_table, e * 4, index_row.astype(F32))
        put_rows(my_table, edges * 4 + e * 4, weight)
    my_table[8 * edges : 8 * edges + 8, :] = jnp.broadcast_to(
        send_ref[...].astype(F32), (8, LANES)
    )

    pick = (
        (
            lax.broadcasted_iota(jnp.int32, (cells, LANES), 0)
            == jnp.broadcast_to(send_ref[...], (cells, LANES))
        )
        .astype(F32)
        .astype(BF16)
    )
    own_high, own_low = split(x_all[:, 0:cells])
    picked = jnp.dot(own_high, pick, preferred_element_type=F32) + jnp.dot(
        own_low, pick, preferred_element_type=F32
    )
    first, second = picked[: 2 * levels], picked[2 * levels :]
    left_wide = lax.broadcasted_iota(jnp.int32, (2 * levels, LANES), 1) < halo
    halo_send[1] = jnp.where(left_wide, first, pltpu.roll(second, halo, 1))
    halo_send[0] = jnp.where(left_wide, pltpu.roll(first, halo, 1), second)

    has_prev = q > 0
    has_next = q < members - 1
    prev_q = jnp.maximum(q - 1, 0)
    next_q = jnp.minimum(q + 1, members - 1)

    pl.semaphore_wait(barrier, greetings)

    def halo_copy(side, target):
        return pltpu.make_async_remote_copy(
            src_ref=halo_send.at[side],
            dst_ref=halo_recv.at[1 - side],
            send_sem=halo_ss.at[side],
            recv_sem=halo_rs.at[1 - side],
            device_id=at(target, lev),
            device_id_type=pl.DeviceIdType.MESH,
        )

    pl.when(has_prev)(lambda: halo_copy(0, prev_q).start())
    pl.when(has_next)(lambda: halo_copy(1, next_q).start())

    def state_copy(i, level, other):
        p, ok = window_partner(i)
        return (
            pltpu.make_async_remote_copy(
                src_ref=state_mine,
                dst_ref=state_all.at[lev, slot_of(q, p)],
                send_sem=state_ss.at[other, i],
                recv_sem=state_rs.at[lev, slot_of(q, p)],
                device_id=at(p, level),
                device_id_type=pl.DeviceIdType.MESH,
            ),
            ok,
        )

    def table_copy(i):
        p, ok = window_partner(i)
        return (
            pltpu.make_async_remote_copy(
                src_ref=table_all.at[mine],
                dst_ref=table_all.at[slot_of(q, p)],
                send_sem=table_ss.at[i],
                recv_sem=table_rs.at[slot_of(q, p)],
                device_id=at(p, lev),
                device_id_type=pl.DeviceIdType.MESH,
            ),
            ok,
        )

    sends = (
        [state_copy(i, 1 - lev, 1) for i in both]
        + [state_copy(i, lev, 0) for i in same]
        + [table_copy(i) for i in same]
    )
    for copy, ok in sends:
        guarded(ok, copy.start)

    state_all[lev, mine] = state_mine[...]

    for e in range(edges):
        for k in range(x_all.shape[1] // LANES):
            ids = lax.broadcasted_iota(jnp.int32, (LANES, cells), 0) + k * LANES
            hot[e, k * LANES : (k + 1) * LANES, :] = (
                (ids == jnp.broadcast_to(near_ref[e : e + 1, :], (LANES, cells)))
                .astype(F32)
                .astype(BF16)
            )
    entry_rows = src_ref.shape[0]
    low_ids = lax.broadcasted_iota(jnp.int32, (LANES, LANES), 0)
    for k in range(entry_rows):
        low = jnp.bitwise_and(loc_ref[k : k + 1, :], LANES - 1)
        flux_hot[:, k * LANES : (k + 1) * LANES] = (
            (low_ids == jnp.broadcast_to(low, (LANES, LANES))).astype(F32).astype(BF16)
        )

    def slot_exists(s):
        if whole:
            return True
        p = q + s - reach
        return (p >= 0) & (p < members)

    pl.when(has_prev)(lambda: halo_copy(1, prev_q).wait_recv())
    pl.when(has_next)(lambda: halo_copy(0, next_q).wait_recv())

    def wait_state(level, s, skip):
        def body():
            pltpu.make_async_remote_copy(
                src_ref=state_mine,
                dst_ref=state_all.at[level, s],
                send_sem=state_ss.at[0, 0],
                recv_sem=state_rs.at[level, s],
                device_id=at(q, 1 - lev),
                device_id_type=pl.DeviceIdType.MESH,
            ).wait_recv()

        ok = slot_exists(s)
        if skip:
            keep = s != mine
            ok = keep if ok is True else keep & ok
        guarded(ok, body)

    for s in range(window):
        wait_state(1 - lev, s, False)
    for s in range(window):
        wait_state(lev, s, True)

    lower_level = lev == 1

    def total_of(slot):
        return pair(state_all[0, slot, 8:16, :])[1]

    def take_listed(value, list_row):
        low = jnp.bitwise_and(list_row, LANES - 1)
        high = jnp.right_shift(list_row, 7)
        got = lanes_of(value, low)
        got = jnp.where(upper & (high == chunk8), got, 0.0)
        return jnp.sum(got, axis=0, keepdims=True)

    def wait_table(s):
        def body():
            pltpu.make_async_remote_copy(
                src_ref=table_all.at[mine],
                dst_ref=table_all.at[s],
                send_sem=table_ss.at[0],
                recv_sem=table_rs.at[s],
                device_id=at(q, 1 - lev),
                device_id_type=pl.DeviceIdType.MESH,
            ).wait_recv()

        ok = slot_exists(s)
        keep = s != mine
        guarded(keep if ok is True else keep & ok, body)

    for s in range(window):
        wait_table(s)

    def list_of(slot):
        return table_all[slot, 8 * edges : 8 * edges + 8, :].astype(jnp.int32)

    above_mine = jnp.where(lower_level, total_of(mine), 0.0)
    above_row = jnp.concatenate([above_mine[c : c + 1, :] for c in range(chunks)], axis=1)
    prev_slot = slot_of(prev_q, q)
    next_slot = slot_of(next_q, q)
    above_halo = jnp.where(
        left8[0:1],
        jnp.where(has_prev, take_listed(total_of(prev_slot), list_of(prev_slot)), 0.0),
        jnp.where(has_next, take_listed(total_of(next_slot), list_of(next_slot)), 0.0),
    )
    above_halo = jnp.where(lower_level, above_halo, 0.0)

    from_prev = jnp.where(has_prev, halo_recv[0], 0.0)
    from_next = jnp.where(has_next, halo_recv[1], 0.0)
    first = jnp.where(left_wide, from_prev, pltpu.roll(from_next, halo, 1))
    second = jnp.where(left_wide, pltpu.roll(from_prev, halo, 1), from_next)
    x_all[0 : 2 * levels, cells:] = first
    x_all[2 * levels : 3 * levels, cells:] = second[:levels]
    x_all[3 * levels :, cells:] = second[levels:] + above_halo
    mont = x_all[3 * levels :, 0:cells] + above_row
    x_all[3 * levels :, 0:cells] = mont
    x_high, x_low = split(x_all[...])
    x_split[0 : 4 * levels, :] = x_high
    x_split[4 * levels :, :] = x_low

    temp_sum = jnp.zeros((levels, cells), F32)
    salt_sum = jnp.zeros((levels, cells), F32)
    rate_sum = jnp.zeros((levels, cells), F32)
    for e in range(edges):
        g = jnp.dot(x_split[...], hot[e], preferred_element_type=F32)
        g = g[: 4 * levels] + g[4 * levels :]
        weight = jnp.where(near_ref[e : e + 1, :] < blank_slot, ew_ref[e : e + 1, :], 0.0)
        step = g[3 * levels :] - mont
        flow = weight * step
        mixed = flow + weight * (2.0 * mixing)
        temp_sum = temp_sum + mixed * (g[:levels] - tr_ref[0])
        salt_sum = salt_sum + mixed * (g[levels : 2 * levels] - tr_ref[1])
        rate_sum = rate_sum + flow * (g[2 * levels : 3 * levels] + th_ref[...])
    temp_new = tr_ref[0] + (0.5 * time_step) * temp_sum
    salt_new = tr_ref[1] + (0.5 * time_step) * salt_sum
    prov = th_ref[...] + (0.5 * time_step) * rate_sum
    tr_out[0] = temp_new
    tr_out[1] = salt_new
    prov_ref[...] = prov
    put_rows(col_mine, 0, jnp.sum(prov, axis=0, keepdims=True))
    put_rows(col_mine, 4, jnp.sum(prov * temp_new, axis=0, keepdims=True))
    put_rows(col_mine, 8, jnp.sum(prov * salt_new, axis=0, keepdims=True))
    put_rows(col_mine, 12, jnp.sum(temp_new, axis=0, keepdims=True))
    put_rows(col_mine, 16, jnp.sum(salt_new, axis=0, keepdims=True))
    col_mine[20:24, :] = jnp.zeros((4, LANES), F32)
    col_copy = pltpu.make_async_remote_copy(
        src_ref=col_mine,
        dst_ref=col_other,
        send_sem=col_ss,
        recv_sem=col_rs,
        device_id=at(q, 1 - lev),
        device_id_type=pl.DeviceIdType.MESH,
    )
    col_copy.start()

    phis, heights, forcings = [], [], []
    for s in range(window):
        height, phi = pair(state_all[0, s, 0:8, :])
        zero_part, zero_total = pair(state_all[0, s, 8:16, :])
        one_part = pair(state_all[1, s, 8:16, :])[0]
        one_thick = pair(state_all[1, s, 16:24, :])[0]
        forcings.append((zero_part + one_part + zero_total * one_thick) / full_levels)
        phis.append(phi)
        heights.append(height)

    def subcycle(step_index, state):
        phis, heights = state
        phis = [p - fast_step * (h + f) for p, h, f in zip(phis, heights, forcings)]
        listed = []
        for s in range(window):
            got = take_listed(phis[s], list_of(s))
            ok = slot_exists(s)
            listed.append(got if ok is True else jnp.where(ok, got, 0.0))
        none = jnp.zeros((1, LANES), F32)
        out = []
        for s in range(window):
            before = listed[s - 1] if s > 0 else none
            after = listed[s + 1] if s < window - 1 else none
            rim = jnp.where(left8[0:1], before, after)
            sources = [
                jnp.broadcast_to(phis[s][c : c + 1, :], (8, LANES)) for c in range(chunks)
            ] + [jnp.broadcast_to(rim, (8, LANES))]
            total = jnp.zeros((8, LANES), F32)
            for j in range(edges // 2):
                index = table_all[s, 8 * j : 8 * j + 8, :].astype(jnp.int32)
                weight = table_all[s, 4 * edges + 8 * j : 4 * edges + 8 * j + 8, :]
                low = jnp.bitwise_and(index, LANES - 1)
                high = jnp.right_shift(index, 7)
                near = jnp.zeros((8, LANES), F32)
                for c, source in enumerate(sources):
                    near = jnp.where(high == c, lanes_of(source, low), near)
                total = total + weight * (near - phis[s])
            total = total + pltpu.roll(total, 4, 0)
            out.append(heights[s] + fast_step * total)
        return phis, out

    phis, heights = lax.fori_loop(0, SUBCYCLES, subcycle, (phis, heights))
    if whole:
        phi_end, ssh_end = phis[0], heights[0]
        for s in range(1, window):
            phi_end = jnp.where(q == s, phis[s], phi_end)
            ssh_end = jnp.where(q == s, heights[s], ssh_end)
    else:
        phi_end, ssh_end = phis[reach], heights[reach]
    ssh_out[...] = ssh_end[0:4, :]

    col_copy.wait_recv()
    column, heat = pair(col_mine[0:8, :] + col_other[0:8, :])
    salt_col, heat_plain = pair(col_mine[8:16, :] + col_other[8:16, :])
    salt_plain = pair(col_mine[16:24, :] + col_other[16:24, :])[0]
    correction = (full_levels + ssh_end - column) / full_levels
    surface = [
        ssh_end,
        phi_end,
        (heat + correction * heat_plain) / full_levels,
        (salt_col + correction * salt_plain) / full_levels,
    ]

    source = src_ref[...]
    low = jnp.bitwise_and(source, LANES - 1)
    high = jnp.right_shift(source, 7)
    contrib = []
    for f in range(4):
        got = jnp.zeros((8, LANES), F32)
        for c in range(chunks):
            row = jnp.broadcast_to(surface[f][c : c + 1, :], (8, LANES))
            got = jnp.where(high == c, lanes_of(row, low), got)
        value = got * rw_ref[...]
        top = value.astype(BF16).astype(F32)
        contrib.append((top, value - top))
    keys = own_ref[...] * 4 + jnp.right_shift(loc_ref[...], 7)
    parts = []
    for k in range(entry_rows):
        pieces = []
        for half in range(2):
            for f in (0, 2):
                one = jnp.broadcast_to(contrib[f][half][k : k + 1, :], (8, LANES))
                two = jnp.broadcast_to(contrib[f + 1][half][k : k + 1, :], (8, LANES))
                pieces.append(jnp.where(upper, one, two))
        parts.append(pieces)

    def fill(p):
        start = p * 16 if isinstance(p, int) else pl.multiple_of(p * 16, 16)
        start_low = start + members * 16
        if not isinstance(p, int):
            start_low = pl.multiple_of(start_low, 16)
        for k in range(entry_rows):
            hit = jnp.broadcast_to(keys[k : k + 1, :], (8, LANES)) == chunk8 + p * 4
            a, b, c, d = [jnp.where(hit, piece, 0.0) for piece in parts[k]]
            lanes = pl.ds(k * LANES, LANES)
            flux_lhs[pl.ds(start, 16), lanes] = jnp.concatenate([a, b], axis=0).astype(BF16)
            flux_lhs[pl.ds(start_low, 16), lanes] = jnp.concatenate([c, d], axis=0).astype(BF16)

    repeat(members, fill)
    block = lax.dot_general(
        flux_lhs[...],
        flux_hot[...],
        (((1,), (1,)), ((), ())),
        preferred_element_type=F32,
    )
    flux_send[...] = (block[: members * 16] + block[members * 16 :]).reshape(members, 16, LANES)

    def flux_copy(i):
        p = lax.rem(q + 1 + i, members)
        return pltpu.make_async_remote_copy(
            src_ref=flux_send.at[p],
            dst_ref=flux_recv.at[q],
            send_sem=flux_ss.at[i],
            recv_sem=flux_rs.at[q],
            device_id=at(p, lev),
            device_id_type=pl.DeviceIdType.MESH,
        )

    repeat(members - 1, lambda i: flux_copy(i).start())
    for c in range(chunks):
        part = slice(c * LANES, (c + 1) * LANES)
        th_out[:, part] = prov_ref[:, part] + correction[c : c + 1, :]

    def flux_arrived(i):
        p = lax.rem(q + 1 + i, members)
        pltpu.make_async_remote_copy(
            src_ref=flux_send.at[p],
            dst_ref=flux_recv.at[p],
            send_sem=flux_ss.at[i],
            recv_sem=flux_rs.at[p],
            device_id=at(p, lev),
            device_id_type=pl.DeviceIdType.MESH,
        ).wait_recv()

    flux_recv[q] = flux_send[q]
    repeat(members - 1, flux_arrived)
    total = jnp.sum(flux_recv[...], axis=0)
    for f in range(4):
        for c in range(chunks):
            atm_out[f : f + 1, c * LANES : (c + 1) * LANES] = total[f * 4 + c : f * 4 + c + 1, :]

    pl.when(has_prev)(lambda: halo_copy(0, prev_q).wait_send())
    pl.when(has_next)(lambda: halo_copy(1, next_q).wait_send())
    for copy, ok in sends:
        guarded(ok, copy.wait_send)
    col_copy.wait_send()
    repeat(members - 1, lambda i: flux_copy(i).wait_send())


def per_device(
    n_cells,
    n_sub,
    tracers,
    thickness,
    ssh,
    potential,
    neighbours,
    edge_weight,
    send_list,
    remap_src,
    remap_owner,
    remap_local,
    remap_weight,
):
    members = n_cells * n_sub
    levels, cells = thickness.shape
    halo = send_list.shape[1]
    edges = neighbours.shape[0]
    entries = remap_src.shape[0]
    reach = SUBCYCLES
    window = members if members <= 2 * reach + 1 else 2 * reach + 1
    rows = entries // LANES
    table_rows = 8 * edges + 8
    wide = cells + 2 * halo
    dma = pltpu.SemaphoreType.DMA
    kernel = functools.partial(ocean_kernel, n_cells, n_sub, reach, window)
    vmem = pl.BlockSpec(memory_space=pltpu.VMEM)
    tr, th, ssh_new, atm = pl.pallas_call(
        kernel,
        out_shape=(
            jax.ShapeDtypeStruct(tracers.shape, F32),
            jax.ShapeDtypeStruct(thickness.shape, F32),
            jax.ShapeDtypeStruct((cells // LANES, LANES), F32),
            jax.ShapeDtypeStruct((4, cells), F32),
        ),
        in_specs=[vmem] * 11,
        out_specs=(vmem,) * 4,
        scratch_shapes=[
            pltpu.VMEM((2, 2 * levels, LANES), F32),
            pltpu.VMEM((2, 2 * levels, LANES), F32),
            pltpu.VMEM((window, table_rows, LANES), F32),
            pltpu.VMEM((24, LANES), F32),
            pltpu.VMEM((2, window, 24, LANES), F32),
            pltpu.VMEM((24, LANES), F32),
            pltpu.VMEM((24, LANES), F32),
            pltpu.VMEM((members, 16, LANES), F32),
            pltpu.VMEM((members, 16, LANES), F32),
            pltpu.VMEM((4 * levels, wide), F32),
            pltpu.VMEM((8 * levels, wide), BF16),
            pltpu.VMEM((edges, wide, cells), BF16),
            pltpu.VMEM((levels, cells), F32),
            pltpu.VMEM((2 * members * 16, entries), BF16),
            pltpu.VMEM((LANES, entries), BF16),
            dma((2,)),
            dma((2,)),
            dma((window,)),
            dma((window,)),
            dma((2, window)),
            dma((2, window)),
            dma,
            dma,
            dma((members,)),
            dma((members,)),
        ],
        compiler_params=pltpu.CompilerParams(
            collective_id=0, has_side_effects=True, vmem_limit_bytes=48 * 1024 * 1024
        ),
        cost_estimate=pl.CostEstimate(
            flops=2 * 8 * levels * wide * cells * edges,
            bytes_accessed=8 * levels * cells * 4,
            transcendentals=0,
        ),
    )(
        tracers,
        thickness,
        ssh.reshape(-1, LANES),
        potential.reshape(-1, LANES),
        neighbours,
        edge_weight,
        jnp.concatenate([send_list[1:2], send_list[0:1]], axis=1),
        remap_src.reshape(rows, LANES),
        remap_owner.reshape(rows, LANES),
        remap_local.reshape(rows, LANES),
        remap_weight.reshape(rows, LANES),
    )
    return tr, th, ssh_new.reshape(cells), atm


def solution(mesh):
    placed = (
        P(None, "lev", ("groups", "cells", "sub")),
        P("lev", ("groups", "cells", "sub")),
        P(("groups", "cells", "sub")),
        P(("groups", "cells", "sub")),
        P(None, ("cells", "sub")),
        P(None, ("cells", "sub")),
        P(None, ("cells", "sub")),
        P(("cells", "sub")),
        P(("cells", "sub"), None),
        P(("cells", "sub")),
        P(("cells", "sub")),
    )
    return jax.shard_map(
        functools.partial(per_device, mesh.shape["cells"], mesh.shape["sub"]),
        mesh=mesh,
        in_specs=placed,
        out_specs=(
            P(None, "lev", ("groups", "cells", "sub")),
            P("lev", ("groups", "cells", "sub")),
            P(("groups", "cells", "sub")),
            P(None, ("groups", "cells", "sub")),
        ),
        check_vma=False,
    )
```

```python
import functools

import jax
import jax.numpy as jnp
from jax import lax
from jax.experimental import pallas as pl
from jax.experimental.pallas import tpu as pltpu
from jax.sharding import PartitionSpec as P

SUBCYCLES = 10

thermal = 0.2
haline = 0.15
time_step = 0.05
mixing = 0.5
fast_step = 0.15

F32 = jnp.float32
BF16 = jnp.bfloat16
LANES = 128


def repeat(count, body):
    if count <= 16:
        for i in range(count):
            body(i)
    else:

        def step(i, carry):
            body(i)
            return carry

        lax.fori_loop(0, count, step, 0)


def guarded(flag, body):
    if flag is True:
        body()
    else:
        pl.when(flag)(body)


def split(x):
    high = x.astype(BF16)
    return high, (x - high.astype(F32)).astype(BF16)


def lanes_of(x, index):
    return jnp.take_along_axis(x, index, axis=1, mode="promise_in_bounds")


def ocean_kernel(
    n_cells,
    n_sub,
    reach,
    window,
    tr_in,
    th_in,
    ssh_in,
    pot_in,
    near_in,
    ew_in,
    list_in,
    src_in,
    own_in,
    loc_in,
    rw_in,
    tr_res,
    th_res,
    ssh_res,
    atm_res,
    halo_send,
    halo_recv,
    table_all,
    state_mine,
    state_all,
    col_mine,
    col_other,
    flux_send,
    flux_recv,
    x_all,
    x_split,
    hot,
    prov_ref,
    flux_lhs,
    flux_hot,
    tr_ref,
    th_ref,
    ssh_ref,
    pot_ref,
    near_ref,
    ew_ref,
    list_ref,
    src_ref,
    own_ref,
    loc_ref,
    rw_ref,
    in_sem,
    tr_out,
    th_out,
    ssh_out,
    atm_out,
    out_sem,
    halo_ss,
    halo_rs,
    table_ss,
    table_rs,
    state_ss,
    state_rs,
    col_ss,
    col_rs,
    flux_ss,
    flux_rs,
):
    members = n_cells * n_sub
    levels, cells = th_ref.shape
    edges = near_ref.shape[0]
    chunks = cells // LANES
    halo = list_ref.shape[1]
    full_levels = 2 * levels
    q = lax.axis_index("cells") * n_sub + lax.axis_index("sub")
    lev = lax.axis_index("lev")
    whole = window == members

    def at(p, level):
        return {"cells": lax.div(p, n_sub), "sub": lax.rem(p, n_sub), "lev": level}

    def slot_of(source, target):
        return source if whole else source - target + reach

    mine = slot_of(q, q)

    def window_partner(i):
        if whole:
            return lax.rem(q + i, members), True
        d = i - reach
        p = q + d
        ok = (p >= 0) & (p < members)
        return jnp.clip(p, 0, members - 1), ok

    same = range(1, members) if whole else [i for i in range(window) if i != reach]
    both = range(window)

    loads = [
        pltpu.make_async_copy(a, b, in_sem.at[i])
        for i, (a, b) in enumerate(
            (
                (tr_in, tr_ref),
                (th_in, th_ref),
                (ssh_in, ssh_ref),
                (pot_in, pot_ref),
                (near_in, near_ref),
                (ew_in, ew_ref),
                (list_in, list_ref),
                (src_in, src_ref),
                (own_in, own_ref),
                (loc_in, loc_ref),
                (rw_in, rw_ref),
            )
        )
    ]
    for copy in loads:
        copy.start()

    results = [
        pltpu.make_async_copy(a, b, out_sem.at[i])
        for i, (a, b) in enumerate(
            ((tr_out, tr_res), (th_out, th_res), (ssh_out, ssh_res), (atm_out, atm_res))
        )
    ]

    barrier = pltpu.get_barrier_semaphore()

    def greet(i):
        p = lax.rem(q + 1 + i, members)
        pl.semaphore_signal(
            barrier, inc=1, device_id=at(p, lev), device_id_type=pl.DeviceIdType.MESH
        )

    repeat(members - 1, greet)
    for i in both:
        p, ok = window_partner(i)
        guarded(
            ok,
            lambda p=p: pl.semaphore_signal(
                barrier, inc=1, device_id=at(p, 1 - lev), device_id_type=pl.DeviceIdType.MESH
            ),
        )
    if whole:
        greetings = members - 1 + window
    else:
        greetings = (
            members
            - 1
            + jnp.minimum(q + reach, members - 1)
            - jnp.maximum(q - reach, 0)
            + 1
        )

    row8 = lax.broadcasted_iota(jnp.int32, (8, LANES), 0)
    lane8 = lax.broadcasted_iota(jnp.int32, (8, LANES), 1)
    upper = row8 < 4
    chunk8 = jnp.where(upper, row8, row8 - 4)
    left8 = lane8 < halo

    def pair(v):
        r = pltpu.roll(v, 4, 0)
        return jnp.where(upper, v, r), jnp.where(upper, r, v)

    def put_rows(ref, start, row):
        for c in range(chunks):
            ref[start + c : start + c + 1, :] = row[:, c * LANES : (c + 1) * LANES]

    for copy in loads:
        copy.wait()
    listed_row = jnp.concatenate([list_ref[1:2, :], list_ref[0:1, :]], axis=1)

    temp = tr_ref[0]
    salt = tr_ref[1]
    thick = th_ref[...]
    load = (thermal * temp - haline * salt) * thick
    rows = lax.broadcasted_iota(jnp.int32, (levels, levels), 0)
    cols = lax.broadcasted_iota(jnp.int32, (levels, levels), 1)
    below = jnp.where(cols < rows, 1.0, jnp.where(cols == rows, 0.5, 0.0)).astype(F32)
    pressure = lax.dot_general(
        below,
        load,
        (((1,), (0,)), ((), ())),
        precision=lax.Precision.HIGHEST,
        preferred_element_type=F32,
    )
    ssh_row = jnp.concatenate([ssh_ref[c : c + 1, :] for c in range(chunks)], axis=1)
    part_mont = pressure + ssh_row
    x_all[0:levels, 0:cells] = temp
    x_all[levels : 2 * levels, 0:cells] = salt
    x_all[2 * levels : 3 * levels, 0:cells] = thick
    x_all[3 * levels : 4 * levels, 0:cells] = part_mont

    state_mine[0:4, :] = ssh_ref[...]
    state_mine[4:8, :] = pot_ref[...]
    put_rows(state_mine, 8, jnp.sum(thick * part_mont, axis=0, keepdims=True))
    put_rows(state_mine, 12, jnp.sum(load, axis=0, keepdims=True))
    put_rows(state_mine, 16, jnp.sum(thick, axis=0, keepdims=True))
    state_mine[20:24, :] = jnp.broadcast_to(listed_row.astype(F32), (4, LANES))

    my_table = table_all.at[mine]
    blank_slot = cells + 2 * halo
    for e in range(edges):
        index_row = near_ref[e : e + 1, :]
        weight = jnp.where(index_row < blank_slot, ew_ref[e : e + 1, :], 0.0)
        put_rows(my_table, e * 4, index_row.astype(F32))
        put_rows(my_table, edges * 4 + e * 4, weight)

    pick = (
        (
            lax.broadcasted_iota(jnp.int32, (cells, LANES), 0)
            == jnp.broadcast_to(listed_row, (cells, LANES))
        )
        .astype(F32)
        .astype(BF16)
    )
    own_high, own_low = split(x_all[:, 0:cells])
    picked = jnp.dot(own_high, pick, preferred_element_type=F32) + jnp.dot(
        own_low, pick, preferred_element_type=F32
    )
    first, second = picked[: 2 * levels], picked[2 * levels :]
    left_wide = lax.broadcasted_iota(jnp.int32, (2 * levels, LANES), 1) < halo
    halo_send[1] = jnp.where(left_wide, first, pltpu.roll(second, halo, 1))
    halo_send[0] = jnp.where(left_wide, pltpu.roll(first, halo, 1), second)

    has_prev = q > 0
    has_next = q < members - 1
    prev_q = jnp.maximum(q - 1, 0)
    next_q = jnp.minimum(q + 1, members - 1)

    pl.semaphore_wait(barrier, greetings)

    def halo_copy(side, target):
        return pltpu.make_async_remote_copy(
            src_ref=halo_send.at[side],
            dst_ref=halo_recv.at[1 - side],
            send_sem=halo_ss.at[side],
            recv_sem=halo_rs.at[1 - side],
            device_id=at(target, lev),
            device_id_type=pl.DeviceIdType.MESH,
        )

    pl.when(has_prev)(lambda: halo_copy(0, prev_q).start())
    pl.when(has_next)(lambda: halo_copy(1, next_q).start())

    def state_copy(i, level, other):
        p, ok = window_partner(i)
        return (
            pltpu.make_async_remote_copy(
                src_ref=state_mine,
                dst_ref=state_all.at[lev, slot_of(q, p)],
                send_sem=state_ss.at[other, i],
                recv_sem=state_rs.at[lev, slot_of(q, p)],
                device_id=at(p, level),
                device_id_type=pl.DeviceIdType.MESH,
            ),
            ok,
        )

    def table_copy(i):
        p, ok = window_partner(i)
        return (
            pltpu.make_async_remote_copy(
                src_ref=table_all.at[mine],
                dst_ref=table_all.at[slot_of(q, p)],
                send_sem=table_ss.at[i],
                recv_sem=table_rs.at[slot_of(q, p)],
                device_id=at(p, lev),
                device_id_type=pl.DeviceIdType.MESH,
            ),
            ok,
        )

    sends = (
        [state_copy(i, 1 - lev, 1) for i in both]
        + [state_copy(i, lev, 0) for i in same]
        + [table_copy(i) for i in same]
    )
    for copy, ok in sends:
        guarded(ok, copy.start)

    state_all[lev, mine] = state_mine[...]

    for e in range(edges):
        for k in range(x_all.shape[1] // LANES):
            ids = lax.broadcasted_iota(jnp.int32, (LANES, cells), 0) + k * LANES
            hot[e, k * LANES : (k + 1) * LANES, :] = (
                (ids == jnp.broadcast_to(near_ref[e : e + 1, :], (LANES, cells)))
                .astype(F32)
                .astype(BF16)
            )
    entry_rows = src_ref.shape[0]
    low_ids = lax.broadcasted_iota(jnp.int32, (LANES, LANES), 0)
    for k in range(entry_rows):
        low = jnp.bitwise_and(loc_ref[k : k + 1, :], LANES - 1)
        flux_hot[:, k * LANES : (k + 1) * LANES] = (
            (low_ids == jnp.broadcast_to(low, (LANES, LANES))).astype(F32).astype(BF16)
        )

    def slot_exists(s):
        if whole:
            return True
        p = q + s - reach
        return (p >= 0) & (p < members)

    pl.when(has_prev)(lambda: halo_copy(1, prev_q).wait_recv())
    pl.when(has_next)(lambda: halo_copy(0, next_q).wait_recv())

    def wait_state(level, s, skip):
        def body():
            pltpu.make_async_remote_copy(
                src_ref=state_mine,
                dst_ref=state_all.at[level, s],
                send_sem=state_ss.at[0, 0],
                recv_sem=state_rs.at[level, s],
                device_id=at(q, 1 - lev),
                device_id_type=pl.DeviceIdType.MESH,
            ).wait_recv()

        ok = slot_exists(s)
        if skip:
            keep = s != mine
            ok = keep if ok is True else keep & ok
        guarded(ok, body)

    for s in range(window):
        wait_state(1 - lev, s, False)
    for s in range(window):
        wait_state(lev, s, True)

    lower_level = lev == 1

    def total_of(slot):
        return pair(state_all[0, slot, 8:16, :])[1]

    def take_listed(value, list_row):
        low = jnp.bitwise_and(list_row, LANES - 1)
        high = jnp.right_shift(list_row, 7)
        got = lanes_of(value, low)
        got = jnp.where(upper & (high == chunk8), got, 0.0)
        return jnp.sum(got, axis=0, keepdims=True)

    def wait_table(s):
        def body():
            pltpu.make_async_remote_copy(
                src_ref=table_all.at[mine],
                dst_ref=table_all.at[s],
                send_sem=table_ss.at[0],
                recv_sem=table_rs.at[s],
                device_id=at(q, 1 - lev),
                device_id_type=pl.DeviceIdType.MESH,
            ).wait_recv()

        ok = slot_exists(s)
        keep = s != mine
        guarded(keep if ok is True else keep & ok, body)

    def list_of(slot):
        return jnp.broadcast_to(
            state_all[0, slot, 20:21, :].astype(jnp.int32), (8, LANES)
        )

    above_mine = jnp.where(lower_level, total_of(mine), 0.0)
    above_row = jnp.concatenate([above_mine[c : c + 1, :] for c in range(chunks)], axis=1)
    prev_slot = slot_of(prev_q, q)
    next_slot = slot_of(next_q, q)
    above_halo = jnp.where(
        left8[0:1],
        jnp.where(has_prev, take_listed(total_of(prev_slot), list_of(prev_slot)), 0.0),
        jnp.where(has_next, take_listed(total_of(next_slot), list_of(next_slot)), 0.0),
    )
    above_halo = jnp.where(lower_level, above_halo, 0.0)

    from_prev = jnp.where(has_prev, halo_recv[0], 0.0)
    from_next = jnp.where(has_next, halo_recv[1], 0.0)
    first = jnp.where(left_wide, from_prev, pltpu.roll(from_next, halo, 1))
    second = jnp.where(left_wide, pltpu.roll(from_prev, halo, 1), from_next)
    x_all[0 : 2 * levels, cells:] = first
    x_all[2 * levels : 3 * levels, cells:] = second[:levels]
    x_all[3 * levels :, cells:] = second[levels:] + above_halo
    mont = x_all[3 * levels :, 0:cells] + above_row
    x_all[3 * levels :, 0:cells] = mont
    x_high, x_low = split(x_all[...])
    x_split[0 : 4 * levels, :] = x_high
    x_split[4 * levels :, :] = x_low

    temp_sum = jnp.zeros((levels, cells), F32)
    salt_sum = jnp.zeros((levels, cells), F32)
    rate_sum = jnp.zeros((levels, cells), F32)
    for e in range(edges):
        g = jnp.dot(x_split[...], hot[e], preferred_element_type=F32)
        g = g[: 4 * levels] + g[4 * levels :]
        weight = jnp.where(near_ref[e : e + 1, :] < blank_slot, ew_ref[e : e + 1, :], 0.0)
        step = g[3 * levels :] - mont
        flow = weight * step
        mixed = flow + weight * (2.0 * mixing)
        temp_sum = temp_sum + mixed * (g[:levels] - tr_ref[0])
        salt_sum = salt_sum + mixed * (g[levels : 2 * levels] - tr_ref[1])
        rate_sum = rate_sum + flow * (g[2 * levels : 3 * levels] + th_ref[...])
    temp_new = tr_ref[0] + (0.5 * time_step) * temp_sum
    salt_new = tr_ref[1] + (0.5 * time_step) * salt_sum
    prov = th_ref[...] + (0.5 * time_step) * rate_sum
    tr_out[0] = temp_new
    tr_out[1] = salt_new
    prov_ref[...] = prov
    put_rows(col_mine, 0, jnp.sum(prov, axis=0, keepdims=True))
    put_rows(col_mine, 4, jnp.sum(prov * temp_new, axis=0, keepdims=True))
    put_rows(col_mine, 8, jnp.sum(prov * salt_new, axis=0, keepdims=True))
    put_rows(col_mine, 12, jnp.sum(temp_new, axis=0, keepdims=True))
    put_rows(col_mine, 16, jnp.sum(salt_new, axis=0, keepdims=True))
    col_mine[20:24, :] = jnp.zeros((4, LANES), F32)
    col_copy = pltpu.make_async_remote_copy(
        src_ref=col_mine,
        dst_ref=col_other,
        send_sem=col_ss,
        recv_sem=col_rs,
        device_id=at(q, 1 - lev),
        device_id_type=pl.DeviceIdType.MESH,
    )
    col_copy.start()
    results[0].start()

    for s in range(window):
        wait_table(s)

    phis, heights, forcings = [], [], []
    for s in range(window):
        height, phi = pair(state_all[0, s, 0:8, :])
        zero_part, zero_total = pair(state_all[0, s, 8:16, :])
        one_part = pair(state_all[1, s, 8:16, :])[0]
        one_thick = pair(state_all[1, s, 16:24, :])[0]
        forcings.append((zero_part + one_part + zero_total * one_thick) / full_levels)
        phis.append(phi)
        heights.append(height)

    def subcycle(step_index, state):
        phis, heights = state
        phis = [p - fast_step * (h + f) for p, h, f in zip(phis, heights, forcings)]
        listed = []
        for s in range(window):
            got = take_listed(phis[s], list_of(s))
            ok = slot_exists(s)
            listed.append(got if ok is True else jnp.where(ok, got, 0.0))
        none = jnp.zeros((1, LANES), F32)
        out = []
        for s in range(window):
            before = listed[s - 1] if s > 0 else none
            after = listed[s + 1] if s < window - 1 else none
            rim = jnp.where(left8[0:1], before, after)
            sources = [
                jnp.broadcast_to(phis[s][c : c + 1, :], (8, LANES)) for c in range(chunks)
            ] + [jnp.broadcast_to(rim, (8, LANES))]
            total = jnp.zeros((8, LANES), F32)
            for j in range(edges // 2):
                index = table_all[s, 8 * j : 8 * j + 8, :].astype(jnp.int32)
                weight = table_all[s, 4 * edges + 8 * j : 4 * edges + 8 * j + 8, :]
                low = jnp.bitwise_and(index, LANES - 1)
                high = jnp.right_shift(index, 7)
                near = jnp.zeros((8, LANES), F32)
                for c, source in enumerate(sources):
                    near = jnp.where(high == c, lanes_of(source, low), near)
                total = total + weight * (near - phis[s])
            total = total + pltpu.roll(total, 4, 0)
            out.append(heights[s] + fast_step * total)
        return phis, out

    phis, heights = lax.fori_loop(0, SUBCYCLES, subcycle, (phis, heights))
    if whole:
        phi_end, ssh_end = phis[0], heights[0]
        for s in range(1, window):
            phi_end = jnp.where(q == s, phis[s], phi_end)
            ssh_end = jnp.where(q == s, heights[s], ssh_end)
    else:
        phi_end, ssh_end = phis[reach], heights[reach]
    ssh_out[...] = ssh_end[0:4, :]
    results[2].start()

    col_copy.wait_recv()
    column, heat = pair(col_mine[0:8, :] + col_other[0:8, :])
    salt_col, heat_plain = pair(col_mine[8:16, :] + col_other[8:16, :])
    salt_plain = pair(col_mine[16:24, :] + col_other[16:24, :])[0]
    correction = (full_levels + ssh_end - column) / full_levels
    surface = [
        ssh_end,
        phi_end,
        (heat + correction * heat_plain) / full_levels,
        (salt_col + correction * salt_plain) / full_levels,
    ]

    source = src_ref[...]
    low = jnp.bitwise_and(source, LANES - 1)
    high = jnp.right_shift(source, 7)
    contrib = []
    for f in range(4):
        got = jnp.zeros((8, LANES), F32)
        for c in range(chunks):
            row = jnp.broadcast_to(surface[f][c : c + 1, :], (8, LANES))
            got = jnp.where(high == c, lanes_of(row, low), got)
        value = got * rw_ref[...]
        top = value.astype(BF16).astype(F32)
        contrib.append((top, value - top))
    keys = own_ref[...] * 4 + jnp.right_shift(loc_ref[...], 7)
    parts = []
    for k in range(entry_rows):
        pieces = []
        for half in range(2):
            for f in (0, 2):
                one = jnp.broadcast_to(contrib[f][half][k : k + 1, :], (8, LANES))
                two = jnp.broadcast_to(contrib[f + 1][half][k : k + 1, :], (8, LANES))
                pieces.append(jnp.where(upper, one, two))
        parts.append(pieces)

    def fill(p):
        start = p * 16 if isinstance(p, int) else pl.multiple_of(p * 16, 16)
        start_low = start + members * 16
        if not isinstance(p, int):
            start_low = pl.multiple_of(start_low, 16)
        for k in range(entry_rows):
            hit = jnp.broadcast_to(keys[k : k + 1, :], (8, LANES)) == chunk8 + p * 4
            a, b, c, d = [jnp.where(hit, piece, 0.0) for piece in parts[k]]
            lanes = pl.ds(k * LANES, LANES)
            flux_lhs[pl.ds(start, 16), lanes] = jnp.concatenate([a, b], axis=0).astype(BF16)
            flux_lhs[pl.ds(start_low, 16), lanes] = jnp.concatenate([c, d], axis=0).astype(BF16)

    repeat(members, fill)
    block = lax.dot_general(
        flux_lhs[...],
        flux_hot[...],
        (((1,), (1,)), ((), ())),
        preferred_element_type=F32,
    )
    flux_send[...] = (block[: members * 16] + block[members * 16 :]).reshape(members, 16, LANES)

    def flux_copy(i):
        p = lax.rem(q + 1 + i, members)
        return pltpu.make_async_remote_copy(
            src_ref=flux_send.at[p],
            dst_ref=flux_recv.at[q],
            send_sem=flux_ss.at[i],
            recv_sem=flux_rs.at[q],
            device_id=at(p, lev),
            device_id_type=pl.DeviceIdType.MESH,
        )

    repeat(members - 1, lambda i: flux_copy(i).start())
    for c in range(chunks):
        part = slice(c * LANES, (c + 1) * LANES)
        th_out[:, part] = prov_ref[:, part] + correction[c : c + 1, :]

    results[1].start()

    def flux_arrived(i):
        p = lax.rem(q + 1 + i, members)
        pltpu.make_async_remote_copy(
            src_ref=flux_send.at[p],
            dst_ref=flux_recv.at[p],
            send_sem=flux_ss.at[i],
            recv_sem=flux_rs.at[p],
            device_id=at(p, lev),
            device_id_type=pl.DeviceIdType.MESH,
        ).wait_recv()

    flux_recv[q] = flux_send[q]
    repeat(members - 1, flux_arrived)
    total = jnp.sum(flux_recv[...], axis=0)
    for f in range(4):
        for c in range(chunks):
            atm_out[f : f + 1, c * LANES : (c + 1) * LANES] = total[f * 4 + c : f * 4 + c + 1, :]

    results[3].start()

    pl.when(has_prev)(lambda: halo_copy(0, prev_q).wait_send())
    pl.when(has_next)(lambda: halo_copy(1, next_q).wait_send())
    for copy, ok in sends:
        guarded(ok, copy.wait_send)
    col_copy.wait_send()
    repeat(members - 1, lambda i: flux_copy(i).wait_send())
    for copy in results:
        copy.wait()


def write_out(*refs):
    sems = refs[-1]
    copies = [
        pltpu.make_async_copy(refs[i], refs[4 + i], sems.at[i]) for i in range(4)
    ]
    for copy in copies:
        copy.start()
    for copy in copies:
        copy.wait()


def per_device(
    n_cells,
    n_sub,
    tracers,
    thickness,
    ssh,
    potential,
    neighbours,
    edge_weight,
    send_list,
    remap_src,
    remap_owner,
    remap_local,
    remap_weight,
):
    members = n_cells * n_sub
    levels, cells = thickness.shape
    halo = send_list.shape[1]
    edges = neighbours.shape[0]
    entries = remap_src.shape[0]
    reach = SUBCYCLES
    window = members if members <= 2 * reach + 1 else 2 * reach + 1
    rows = entries // LANES
    table_rows = 8 * edges
    wide = cells + 2 * halo
    dma = pltpu.SemaphoreType.DMA
    kernel = functools.partial(ocean_kernel, n_cells, n_sub, reach, window)
    hbm = pl.BlockSpec(memory_space=pltpu.HBM)
    tr, th, ssh_new, atm = pl.pallas_call(
        kernel,
        out_shape=(
            jax.ShapeDtypeStruct(tracers.shape, F32),
            jax.ShapeDtypeStruct(thickness.shape, F32),
            jax.ShapeDtypeStruct((cells // LANES, LANES), F32),
            jax.ShapeDtypeStruct((4, cells), F32),
        ),
        in_specs=[hbm] * 11,
        out_specs=(hbm,) * 4,
        scratch_shapes=[
            pltpu.VMEM((2, 2 * levels, LANES), F32),
            pltpu.VMEM((2, 2 * levels, LANES), F32),
            pltpu.VMEM((window, table_rows, LANES), F32),
            pltpu.VMEM((24, LANES), F32),
            pltpu.VMEM((2, window, 24, LANES), F32),
            pltpu.VMEM((24, LANES), F32),
            pltpu.VMEM((24, LANES), F32),
            pltpu.VMEM((members, 16, LANES), F32),
            pltpu.VMEM((members, 16, LANES), F32),
            pltpu.VMEM((4 * levels, wide), F32),
            pltpu.VMEM((8 * levels, wide), BF16),
            pltpu.VMEM((edges, wide, cells), BF16),
            pltpu.VMEM((levels, cells), F32),
            pltpu.VMEM((2 * members * 16, entries), BF16),
            pltpu.VMEM((LANES, entries), BF16),
            pltpu.VMEM(tracers.shape, F32),
            pltpu.VMEM(thickness.shape, F32),
            pltpu.VMEM((cells // LANES, LANES), F32),
            pltpu.VMEM((cells // LANES, LANES), F32),
            pltpu.VMEM(neighbours.shape, jnp.int32),
            pltpu.VMEM(neighbours.shape, F32),
            pltpu.VMEM(send_list.shape, jnp.int32),
            pltpu.VMEM((rows, LANES), jnp.int32),
            pltpu.VMEM((rows, LANES), jnp.int32),
            pltpu.VMEM((rows, LANES), jnp.int32),
            pltpu.VMEM((rows, LANES), F32),
            dma((11,)),
            pltpu.VMEM(tracers.shape, F32),
            pltpu.VMEM(thickness.shape, F32),
            pltpu.VMEM((cells // LANES, LANES), F32),
            pltpu.VMEM((4, cells), F32),
            dma((4,)),
            dma((2,)),
            dma((2,)),
            dma((window,)),
            dma((window,)),
            dma((2, window)),
            dma((2, window)),
            dma,
            dma,
            dma((members,)),
            dma((members,)),
        ],
        compiler_params=pltpu.CompilerParams(
            collective_id=0, has_side_effects=True, vmem_limit_bytes=60 * 1024 * 1024
        ),
        cost_estimate=pl.CostEstimate(
            flops=2 * 8 * levels * wide * cells * edges,
            bytes_accessed=8 * levels * cells * 4,
            transcendentals=0,
        ),
    )(
        tracers,
        thickness,
        ssh.reshape(-1, LANES),
        potential.reshape(-1, LANES),
        neighbours,
        edge_weight,
        send_list,
        remap_src.reshape(rows, LANES),
        remap_owner.reshape(rows, LANES),
        remap_local.reshape(rows, LANES),
        remap_weight.reshape(rows, LANES),
    )
    tr, th, ssh_new, atm = pl.pallas_call(
        write_out,
        out_shape=tuple(jax.ShapeDtypeStruct(a.shape, F32) for a in (tr, th, ssh_new, atm)),
        in_specs=[hbm] * 4,
        out_specs=(hbm,) * 4,
        scratch_shapes=[dma((4,))],
        compiler_params=pltpu.CompilerParams(vmem_limit_bytes=60 * 1024 * 1024),
    )(tr, th, ssh_new, atm)
    return tr, th, ssh_new.reshape(cells), atm


def solution(mesh):
    placed = (
        P(None, "lev", ("groups", "cells", "sub")),
        P("lev", ("groups", "cells", "sub")),
        P(("groups", "cells", "sub")),
        P(("groups", "cells", "sub")),
        P(None, ("cells", "sub")),
        P(None, ("cells", "sub")),
        P(None, ("cells", "sub")),
        P(("cells", "sub")),
        P(("cells", "sub"), None),
        P(("cells", "sub")),
        P(("cells", "sub")),
    )
    return jax.shard_map(
        functools.partial(per_device, mesh.shape["cells"], mesh.shape["sub"]),
        mesh=mesh,
        in_specs=placed,
        out_specs=(
            P(None, "lev", ("groups", "cells", "sub")),
            P("lev", ("groups", "cells", "sub")),
            P(("groups", "cells", "sub")),
            P(None, ("groups", "cells", "sub")),
        ),
        check_vma=False,
    )
```

```python
import functools

import jax
import jax.numpy as jnp
from jax import lax
from jax.experimental import pallas as pl
from jax.experimental.pallas import tpu as pltpu
from jax.sharding import PartitionSpec as P

SUBCYCLES = 10

thermal = 0.2
haline = 0.15
time_step = 0.05
mixing = 0.5
fast_step = 0.15

F32 = jnp.float32
BF16 = jnp.bfloat16
LANES = 128


def repeat(count, body):
    if count <= 16:
        for i in range(count):
            body(i)
    else:

        def step(i, carry):
            body(i)
            return carry

        lax.fori_loop(0, count, step, 0)


def guarded(flag, body):
    if flag is True:
        body()
    else:
        pl.when(flag)(body)


def split(x):
    high = x.astype(BF16)
    return high, (x - high.astype(F32)).astype(BF16)


def lanes_of(x, index):
    return jnp.take_along_axis(x, index, axis=1, mode="promise_in_bounds")


def ocean_kernel(
    n_cells,
    n_sub,
    reach,
    window,
    tr_in,
    th_in,
    ssh_in,
    pot_in,
    near_in,
    ew_in,
    list_in,
    src_in,
    own_in,
    loc_in,
    rw_in,
    tr_res,
    th_res,
    ssh_res,
    atm_res,
    halo_send,
    halo_recv,
    table_all,
    state_mine,
    state_all,
    col_mine,
    col_other,
    flux_send,
    flux_recv,
    x_all,
    x_split,
    hot,
    prov_ref,
    flux_lhs,
    flux_hot,
    tr_ref,
    th_ref,
    ssh_ref,
    pot_ref,
    near_ref,
    ew_ref,
    list_ref,
    src_ref,
    own_ref,
    loc_ref,
    rw_ref,
    in_sem,
    tr_out,
    th_out,
    ssh_out,
    atm_out,
    out_sem,
    halo_ss,
    halo_rs,
    table_ss,
    table_rs,
    state_ss,
    state_rs,
    col_ss,
    col_rs,
    flux_ss,
    flux_rs,
):
    members = n_cells * n_sub
    levels, cells = th_ref.shape
    edges = near_ref.shape[0]
    chunks = cells // LANES
    halo = list_ref.shape[1]
    full_levels = 2 * levels
    q = lax.axis_index("cells") * n_sub + lax.axis_index("sub")
    lev = lax.axis_index("lev")
    whole = window == members

    def at(p, level):
        return {"cells": lax.div(p, n_sub), "sub": lax.rem(p, n_sub), "lev": level}

    def slot_of(source, target):
        return source if whole else source - target + reach

    mine = slot_of(q, q)

    def window_partner(i):
        if whole:
            return lax.rem(q + i, members), True
        d = i - reach
        p = q + d
        ok = (p >= 0) & (p < members)
        return jnp.clip(p, 0, members - 1), ok

    same = range(1, members) if whole else [i for i in range(window) if i != reach]
    both = range(window)

    loads = [
        pltpu.make_async_copy(a, b, in_sem.at[i])
        for i, (a, b) in enumerate(
            (
                (tr_in, tr_ref),
                (th_in, th_ref),
                (ssh_in, ssh_ref),
                (pot_in, pot_ref),
                (near_in, near_ref),
                (ew_in, ew_ref),
                (list_in, list_ref),
                (src_in, src_ref),
                (own_in, own_ref),
                (loc_in, loc_ref),
                (rw_in, rw_ref),
            )
        )
    ]
    for copy in loads:
        copy.start()

    results = [
        pltpu.make_async_copy(a, b, out_sem.at[i])
        for i, (a, b) in enumerate(
            ((tr_out, tr_res), (th_out, th_res), (ssh_out, ssh_res), (atm_out, atm_res))
        )
    ]

    barrier = pltpu.get_barrier_semaphore()

    def greet(i):
        p = lax.rem(q + 1 + i, members)
        pl.semaphore_signal(
            barrier, inc=1, device_id=at(p, lev), device_id_type=pl.DeviceIdType.MESH
        )

    repeat(members - 1, greet)
    for i in both:
        p, ok = window_partner(i)
        guarded(
            ok,
            lambda p=p: pl.semaphore_signal(
                barrier, inc=1, device_id=at(p, 1 - lev), device_id_type=pl.DeviceIdType.MESH
            ),
        )
    if whole:
        greetings = members - 1 + window
    else:
        greetings = (
            members
            - 1
            + jnp.minimum(q + reach, members - 1)
            - jnp.maximum(q - reach, 0)
            + 1
        )

    row8 = lax.broadcasted_iota(jnp.int32, (8, LANES), 0)
    lane8 = lax.broadcasted_iota(jnp.int32, (8, LANES), 1)
    upper = row8 < 4
    chunk8 = jnp.where(upper, row8, row8 - 4)
    left8 = lane8 < halo

    def pair(v):
        r = pltpu.roll(v, 4, 0)
        return jnp.where(upper, v, r), jnp.where(upper, r, v)

    def put_rows(ref, start, row):
        for c in range(chunks):
            ref[start + c : start + c + 1, :] = row[:, c * LANES : (c + 1) * LANES]

    for copy in loads:
        copy.wait()
    listed_row = jnp.concatenate([list_ref[1:2, :], list_ref[0:1, :]], axis=1)

    temp = tr_ref[0]
    salt = tr_ref[1]
    thick = th_ref[...]
    load = (thermal * temp - haline * salt) * thick
    rows = lax.broadcasted_iota(jnp.int32, (levels, levels), 0)
    cols = lax.broadcasted_iota(jnp.int32, (levels, levels), 1)
    below = jnp.where(cols < rows, 1.0, jnp.where(cols == rows, 0.5, 0.0)).astype(F32)
    pressure = lax.dot_general(
        below,
        load,
        (((1,), (0,)), ((), ())),
        precision=lax.Precision.HIGHEST,
        preferred_element_type=F32,
    )
    ssh_row = jnp.concatenate([ssh_ref[c : c + 1, :] for c in range(chunks)], axis=1)
    part_mont = pressure + ssh_row
    x_all[0:levels, 0:cells] = temp
    x_all[levels : 2 * levels, 0:cells] = salt
    x_all[2 * levels : 3 * levels, 0:cells] = thick
    x_all[3 * levels : 4 * levels, 0:cells] = part_mont

    state_mine[0:4, :] = ssh_ref[...]
    state_mine[4:8, :] = pot_ref[...]
    put_rows(state_mine, 8, jnp.sum(thick * part_mont, axis=0, keepdims=True))
    put_rows(state_mine, 12, jnp.sum(load, axis=0, keepdims=True))
    put_rows(state_mine, 16, jnp.sum(thick, axis=0, keepdims=True))
    state_mine[20:24, :] = jnp.broadcast_to(listed_row.astype(F32), (4, LANES))

    my_table = table_all.at[mine]
    blank_slot = cells + 2 * halo
    for e in range(edges):
        index_row = near_ref[e : e + 1, :]
        weight = jnp.where(index_row < blank_slot, ew_ref[e : e + 1, :], 0.0)
        put_rows(my_table, e * 4, index_row.astype(F32))
        put_rows(my_table, edges * 4 + e * 4, weight)

    pick = (
        (
            lax.broadcasted_iota(jnp.int32, (cells, LANES), 0)
            == jnp.broadcast_to(listed_row, (cells, LANES))
        )
        .astype(F32)
        .astype(BF16)
    )
    own_high, own_low = split(x_all[:, 0:cells])
    picked = jnp.dot(own_high, pick, preferred_element_type=F32) + jnp.dot(
        own_low, pick, preferred_element_type=F32
    )
    first, second = picked[: 2 * levels], picked[2 * levels :]
    left_wide = lax.broadcasted_iota(jnp.int32, (2 * levels, LANES), 1) < halo
    halo_send[1] = jnp.where(left_wide, first, pltpu.roll(second, halo, 1))
    halo_send[0] = jnp.where(left_wide, pltpu.roll(first, halo, 1), second)

    has_prev = q > 0
    has_next = q < members - 1
    prev_q = jnp.maximum(q - 1, 0)
    next_q = jnp.minimum(q + 1, members - 1)

    pl.semaphore_wait(barrier, greetings)

    def halo_copy(side, target):
        return pltpu.make_async_remote_copy(
            src_ref=halo_send.at[side],
            dst_ref=halo_recv.at[1 - side],
            send_sem=halo_ss.at[side],
            recv_sem=halo_rs.at[1 - side],
            device_id=at(target, lev),
            device_id_type=pl.DeviceIdType.MESH,
        )

    pl.when(has_prev)(lambda: halo_copy(0, prev_q).start())
    pl.when(has_next)(lambda: halo_copy(1, next_q).start())

    def state_copy(i, level, other):
        p, ok = window_partner(i)
        return (
            pltpu.make_async_remote_copy(
                src_ref=state_mine,
                dst_ref=state_all.at[lev, slot_of(q, p)],
                send_sem=state_ss.at[other, i],
                recv_sem=state_rs.at[lev, slot_of(q, p)],
                device_id=at(p, level),
                device_id_type=pl.DeviceIdType.MESH,
            ),
            ok,
        )

    def table_copy(i):
        p, ok = window_partner(i)
        return (
            pltpu.make_async_remote_copy(
                src_ref=table_all.at[mine],
                dst_ref=table_all.at[slot_of(q, p)],
                send_sem=table_ss.at[i],
                recv_sem=table_rs.at[slot_of(q, p)],
                device_id=at(p, lev),
                device_id_type=pl.DeviceIdType.MESH,
            ),
            ok,
        )

    sends = (
        [state_copy(i, 1 - lev, 1) for i in both]
        + [state_copy(i, lev, 0) for i in same]
        + [table_copy(i) for i in same]
    )
    for copy, ok in sends:
        guarded(ok, copy.start)

    state_all[lev, mine] = state_mine[...]

    for e in range(edges):
        for k in range(x_all.shape[1] // LANES):
            ids = lax.broadcasted_iota(jnp.int32, (LANES, cells), 0) + k * LANES
            hot[e, k * LANES : (k + 1) * LANES, :] = (
                (ids == jnp.broadcast_to(near_ref[e : e + 1, :], (LANES, cells)))
                .astype(F32)
                .astype(BF16)
            )
    entry_rows = src_ref.shape[0]
    low_ids = lax.broadcasted_iota(jnp.int32, (LANES, LANES), 0)
    for k in range(entry_rows):
        low = jnp.bitwise_and(loc_ref[k : k + 1, :], LANES - 1)
        flux_hot[:, k * LANES : (k + 1) * LANES] = (
            (low_ids == jnp.broadcast_to(low, (LANES, LANES))).astype(F32).astype(BF16)
        )

    def slot_exists(s):
        if whole:
            return True
        p = q + s - reach
        return (p >= 0) & (p < members)

    pl.when(has_prev)(lambda: halo_copy(1, prev_q).wait_recv())
    pl.when(has_next)(lambda: halo_copy(0, next_q).wait_recv())

    def wait_state(level, s, skip):
        def body():
            pltpu.make_async_remote_copy(
                src_ref=state_mine,
                dst_ref=state_all.at[level, s],
                send_sem=state_ss.at[0, 0],
                recv_sem=state_rs.at[level, s],
                device_id=at(q, 1 - lev),
                device_id_type=pl.DeviceIdType.MESH,
            ).wait_recv()

        ok = slot_exists(s)
        if skip:
            keep = s != mine
            ok = keep if ok is True else keep & ok
        guarded(ok, body)

    for s in range(window):
        wait_state(1 - lev, s, False)
    for s in range(window):
        wait_state(lev, s, True)

    lower_level = lev == 1

    def total_of(slot):
        return pair(state_all[0, slot, 8:16, :])[1]

    def take_listed(value, list_row):
        low = jnp.bitwise_and(list_row, LANES - 1)
        high = jnp.right_shift(list_row, 7)
        got = lanes_of(value, low)
        got = jnp.where(upper & (high == chunk8), got, 0.0)
        return jnp.sum(got, axis=0, keepdims=True)

    def wait_table(s):
        def body():
            pltpu.make_async_remote_copy(
                src_ref=table_all.at[mine],
                dst_ref=table_all.at[s],
                send_sem=table_ss.at[0],
                recv_sem=table_rs.at[s],
                device_id=at(q, 1 - lev),
                device_id_type=pl.DeviceIdType.MESH,
            ).wait_recv()

        ok = slot_exists(s)
        keep = s != mine
        guarded(keep if ok is True else keep & ok, body)

    def list_of(slot):
        return jnp.broadcast_to(
            state_all[0, slot, 20:21, :].astype(jnp.int32), (8, LANES)
        )

    above_mine = jnp.where(lower_level, total_of(mine), 0.0)
    above_row = jnp.concatenate([above_mine[c : c + 1, :] for c in range(chunks)], axis=1)
    prev_slot = slot_of(prev_q, q)
    next_slot = slot_of(next_q, q)
    above_halo = jnp.where(
        left8[0:1],
        jnp.where(has_prev, take_listed(total_of(prev_slot), list_of(prev_slot)), 0.0),
        jnp.where(has_next, take_listed(total_of(next_slot), list_of(next_slot)), 0.0),
    )
    above_halo = jnp.where(lower_level, above_halo, 0.0)

    from_prev = jnp.where(has_prev, halo_recv[0], 0.0)
    from_next = jnp.where(has_next, halo_recv[1], 0.0)
    first = jnp.where(left_wide, from_prev, pltpu.roll(from_next, halo, 1))
    second = jnp.where(left_wide, pltpu.roll(from_prev, halo, 1), from_next)
    x_all[0 : 2 * levels, cells:] = first
    x_all[2 * levels : 3 * levels, cells:] = second[:levels]
    x_all[3 * levels :, cells:] = second[levels:] + above_halo
    mont = x_all[3 * levels :, 0:cells] + above_row
    x_all[3 * levels :, 0:cells] = mont
    x_high, x_low = split(x_all[...])
    x_split[0 : 4 * levels, :] = x_high
    x_split[4 * levels :, :] = x_low

    temp_sum = jnp.zeros((levels, cells), F32)
    salt_sum = jnp.zeros((levels, cells), F32)
    rate_sum = jnp.zeros((levels, cells), F32)
    for e in range(edges):
        g = jnp.dot(x_split[...], hot[e], preferred_element_type=F32)
        g = g[: 4 * levels] + g[4 * levels :]
        weight = jnp.where(near_ref[e : e + 1, :] < blank_slot, ew_ref[e : e + 1, :], 0.0)
        step = g[3 * levels :] - mont
        flow = weight * step
        mixed = flow + weight * (2.0 * mixing)
        temp_sum = temp_sum + mixed * (g[:levels] - tr_ref[0])
        salt_sum = salt_sum + mixed * (g[levels : 2 * levels] - tr_ref[1])
        rate_sum = rate_sum + flow * (g[2 * levels : 3 * levels] + th_ref[...])
    temp_new = tr_ref[0] + (0.5 * time_step) * temp_sum
    salt_new = tr_ref[1] + (0.5 * time_step) * salt_sum
    prov = th_ref[...] + (0.5 * time_step) * rate_sum
    tr_out[0] = temp_new
    tr_out[1] = salt_new
    prov_ref[...] = prov
    put_rows(col_mine, 0, jnp.sum(prov, axis=0, keepdims=True))
    put_rows(col_mine, 4, jnp.sum(prov * temp_new, axis=0, keepdims=True))
    put_rows(col_mine, 8, jnp.sum(prov * salt_new, axis=0, keepdims=True))
    put_rows(col_mine, 12, jnp.sum(temp_new, axis=0, keepdims=True))
    put_rows(col_mine, 16, jnp.sum(salt_new, axis=0, keepdims=True))
    col_mine[20:24, :] = jnp.zeros((4, LANES), F32)
    col_copy = pltpu.make_async_remote_copy(
        src_ref=col_mine,
        dst_ref=col_other,
        send_sem=col_ss,
        recv_sem=col_rs,
        device_id=at(q, 1 - lev),
        device_id_type=pl.DeviceIdType.MESH,
    )
    col_copy.start()
    results[0].start()

    for s in range(window):
        wait_table(s)

    phis, heights, forcings = [], [], []
    for s in range(window):
        height, phi = pair(state_all[0, s, 0:8, :])
        zero_part, zero_total = pair(state_all[0, s, 8:16, :])
        one_part = pair(state_all[1, s, 8:16, :])[0]
        one_thick = pair(state_all[1, s, 16:24, :])[0]
        forcings.append((zero_part + one_part + zero_total * one_thick) / full_levels)
        phis.append(phi)
        heights.append(height)

    def subcycle(step_index, state):
        phis, heights = state
        phis = [p - fast_step * (h + f) for p, h, f in zip(phis, heights, forcings)]
        listed = []
        for s in range(window):
            got = take_listed(phis[s], list_of(s))
            ok = slot_exists(s)
            listed.append(got if ok is True else jnp.where(ok, got, 0.0))
        none = jnp.zeros((1, LANES), F32)
        out = []
        for s in range(window):
            before = listed[s - 1] if s > 0 else none
            after = listed[s + 1] if s < window - 1 else none
            rim = jnp.where(left8[0:1], before, after)
            sources = [
                jnp.broadcast_to(phis[s][c : c + 1, :], (8, LANES)) for c in range(chunks)
            ] + [jnp.broadcast_to(rim, (8, LANES))]
            total = jnp.zeros((8, LANES), F32)
            for j in range(edges // 2):
                index = table_all[s, 8 * j : 8 * j + 8, :].astype(jnp.int32)
                weight = table_all[s, 4 * edges + 8 * j : 4 * edges + 8 * j + 8, :]
                low = jnp.bitwise_and(index, LANES - 1)
                high = jnp.right_shift(index, 7)
                near = jnp.zeros((8, LANES), F32)
                for c, source in enumerate(sources):
                    near = jnp.where(high == c, lanes_of(source, low), near)
                total = total + weight * (near - phis[s])
            total = total + pltpu.roll(total, 4, 0)
            out.append(heights[s] + fast_step * total)
        return phis, out

    phis, heights = lax.fori_loop(0, SUBCYCLES, subcycle, (phis, heights))
    if whole:
        phi_end, ssh_end = phis[0], heights[0]
        for s in range(1, window):
            phi_end = jnp.where(q == s, phis[s], phi_end)
            ssh_end = jnp.where(q == s, heights[s], ssh_end)
    else:
        phi_end, ssh_end = phis[reach], heights[reach]
    ssh_out[...] = ssh_end[0:4, :]
    results[2].start()

    col_copy.wait_recv()
    column, heat = pair(col_mine[0:8, :] + col_other[0:8, :])
    salt_col, heat_plain = pair(col_mine[8:16, :] + col_other[8:16, :])
    salt_plain = pair(col_mine[16:24, :] + col_other[16:24, :])[0]
    correction = (full_levels + ssh_end - column) / full_levels
    surface = [
        ssh_end,
        phi_end,
        (heat + correction * heat_plain) / full_levels,
        (salt_col + correction * salt_plain) / full_levels,
    ]

    source = src_ref[...]
    low = jnp.bitwise_and(source, LANES - 1)
    high = jnp.right_shift(source, 7)
    contrib = []
    for f in range(4):
        got = jnp.zeros((8, LANES), F32)
        for c in range(chunks):
            row = jnp.broadcast_to(surface[f][c : c + 1, :], (8, LANES))
            got = jnp.where(high == c, lanes_of(row, low), got)
        value = got * rw_ref[...]
        top = value.astype(BF16).astype(F32)
        contrib.append((top, value - top))
    keys = own_ref[...] * 4 + jnp.right_shift(loc_ref[...], 7)
    parts = []
    for k in range(entry_rows):
        pieces = []
        for half in range(2):
            for f in (0, 2):
                one = jnp.broadcast_to(contrib[f][half][k : k + 1, :], (8, LANES))
                two = jnp.broadcast_to(contrib[f + 1][half][k : k + 1, :], (8, LANES))
                pieces.append(jnp.where(upper, one, two))
        parts.append(pieces)

    def fill(p):
        start = p * 16 if isinstance(p, int) else pl.multiple_of(p * 16, 16)
        start_low = start + members * 16
        if not isinstance(p, int):
            start_low = pl.multiple_of(start_low, 16)
        for k in range(entry_rows):
            hit = jnp.broadcast_to(keys[k : k + 1, :], (8, LANES)) == chunk8 + p * 4
            a, b, c, d = [jnp.where(hit, piece, 0.0) for piece in parts[k]]
            lanes = pl.ds(k * LANES, LANES)
            flux_lhs[pl.ds(start, 16), lanes] = jnp.concatenate([a, b], axis=0).astype(BF16)
            flux_lhs[pl.ds(start_low, 16), lanes] = jnp.concatenate([c, d], axis=0).astype(BF16)

    repeat(members, fill)
    block = lax.dot_general(
        flux_lhs[...],
        flux_hot[...],
        (((1,), (1,)), ((), ())),
        preferred_element_type=F32,
    )
    flux_send[...] = (block[: members * 16] + block[members * 16 :]).reshape(members, 16, LANES)

    def flux_copy(i):
        p = lax.rem(q + 1 + i, members)
        return pltpu.make_async_remote_copy(
            src_ref=flux_send.at[p],
            dst_ref=flux_recv.at[q],
            send_sem=flux_ss.at[i],
            recv_sem=flux_rs.at[q],
            device_id=at(p, lev),
            device_id_type=pl.DeviceIdType.MESH,
        )

    repeat(members - 1, lambda i: flux_copy(i).start())
    for c in range(chunks):
        part = slice(c * LANES, (c + 1) * LANES)
        th_out[:, part] = prov_ref[:, part] + correction[c : c + 1, :]

    results[1].start()

    def flux_arrived(i):
        p = lax.rem(q + 1 + i, members)
        pltpu.make_async_remote_copy(
            src_ref=flux_send.at[p],
            dst_ref=flux_recv.at[p],
            send_sem=flux_ss.at[i],
            recv_sem=flux_rs.at[p],
            device_id=at(p, lev),
            device_id_type=pl.DeviceIdType.MESH,
        ).wait_recv()

    flux_recv[q] = flux_send[q]
    repeat(members - 1, flux_arrived)
    total = jnp.sum(flux_recv[...], axis=0)
    for f in range(4):
        for c in range(chunks):
            atm_out[f : f + 1, c * LANES : (c + 1) * LANES] = total[f * 4 + c : f * 4 + c + 1, :]

    results[3].start()

    pl.when(has_prev)(lambda: halo_copy(0, prev_q).wait_send())
    pl.when(has_next)(lambda: halo_copy(1, next_q).wait_send())
    for copy, ok in sends:
        guarded(ok, copy.wait_send)
    col_copy.wait_send()
    repeat(members - 1, lambda i: flux_copy(i).wait_send())
    for copy in results:
        copy.wait()


def write_out(*refs):
    in_sem, out_sem = refs[12:]
    fetch = [pltpu.make_async_copy(refs[i], refs[8 + i], in_sem.at[i]) for i in range(4)]
    store = [pltpu.make_async_copy(refs[8 + i], refs[4 + i], out_sem.at[i]) for i in range(4)]
    for copy in fetch:
        copy.start()
    for i in range(4):
        fetch[i].wait()
        store[i].start()
    for copy in store:
        copy.wait()


def per_device(
    n_cells,
    n_sub,
    tracers,
    thickness,
    ssh,
    potential,
    neighbours,
    edge_weight,
    send_list,
    remap_src,
    remap_owner,
    remap_local,
    remap_weight,
):
    members = n_cells * n_sub
    levels, cells = thickness.shape
    halo = send_list.shape[1]
    edges = neighbours.shape[0]
    entries = remap_src.shape[0]
    reach = SUBCYCLES
    window = members if members <= 2 * reach + 1 else 2 * reach + 1
    rows = entries // LANES
    table_rows = 8 * edges
    wide = cells + 2 * halo
    dma = pltpu.SemaphoreType.DMA
    kernel = functools.partial(ocean_kernel, n_cells, n_sub, reach, window)
    hbm = pl.BlockSpec(memory_space=pltpu.HBM)
    tr, th, ssh_new, atm = pl.pallas_call(
        kernel,
        out_shape=(
            jax.ShapeDtypeStruct(tracers.shape, F32),
            jax.ShapeDtypeStruct(thickness.shape, F32),
            jax.ShapeDtypeStruct((cells // LANES, LANES), F32),
            jax.ShapeDtypeStruct((4, cells), F32),
        ),
        in_specs=[hbm] * 11,
        out_specs=(hbm,) * 4,
        scratch_shapes=[
            pltpu.VMEM((2, 2 * levels, LANES), F32),
            pltpu.VMEM((2, 2 * levels, LANES), F32),
            pltpu.VMEM((window, table_rows, LANES), F32),
            pltpu.VMEM((24, LANES), F32),
            pltpu.VMEM((2, window, 24, LANES), F32),
            pltpu.VMEM((24, LANES), F32),
            pltpu.VMEM((24, LANES), F32),
            pltpu.VMEM((members, 16, LANES), F32),
            pltpu.VMEM((members, 16, LANES), F32),
            pltpu.VMEM((4 * levels, wide), F32),
            pltpu.VMEM((8 * levels, wide), BF16),
            pltpu.VMEM((edges, wide, cells), BF16),
            pltpu.VMEM((levels, cells), F32),
            pltpu.VMEM((2 * members * 16, entries), BF16),
            pltpu.VMEM((LANES, entries), BF16),
            pltpu.VMEM(tracers.shape, F32),
            pltpu.VMEM(thickness.shape, F32),
            pltpu.VMEM((cells // LANES, LANES), F32),
            pltpu.VMEM((cells // LANES, LANES), F32),
            pltpu.VMEM(neighbours.shape, jnp.int32),
            pltpu.VMEM(neighbours.shape, F32),
            pltpu.VMEM(send_list.shape, jnp.int32),
            pltpu.VMEM((rows, LANES), jnp.int32),
            pltpu.VMEM((rows, LANES), jnp.int32),
            pltpu.VMEM((rows, LANES), jnp.int32),
            pltpu.VMEM((rows, LANES), F32),
            dma((11,)),
            pltpu.VMEM(tracers.shape, F32),
            pltpu.VMEM(thickness.shape, F32),
            pltpu.VMEM((cells // LANES, LANES), F32),
            pltpu.VMEM((4, cells), F32),
            dma((4,)),
            dma((2,)),
            dma((2,)),
            dma((window,)),
            dma((window,)),
            dma((2, window)),
            dma((2, window)),
            dma,
            dma,
            dma((members,)),
            dma((members,)),
        ],
        compiler_params=pltpu.CompilerParams(
            collective_id=0, has_side_effects=True, vmem_limit_bytes=60 * 1024 * 1024
        ),
        cost_estimate=pl.CostEstimate(
            flops=2 * 8 * levels * wide * cells * edges,
            bytes_accessed=8 * levels * cells * 4,
            transcendentals=0,
        ),
    )(
        tracers,
        thickness,
        ssh.reshape(-1, LANES),
        potential.reshape(-1, LANES),
        neighbours,
        edge_weight,
        send_list,
        remap_src.reshape(rows, LANES),
        remap_owner.reshape(rows, LANES),
        remap_local.reshape(rows, LANES),
        remap_weight.reshape(rows, LANES),
    )
    tr, th, ssh_new, atm = pl.pallas_call(
        write_out,
        out_shape=tuple(jax.ShapeDtypeStruct(a.shape, F32) for a in (tr, th, ssh_new, atm)),
        in_specs=[hbm] * 4,
        out_specs=(hbm,) * 4,
        scratch_shapes=[pltpu.VMEM(a.shape, F32) for a in (tr, th, ssh_new, atm)]
        + [dma((4,)), dma((4,))],
        compiler_params=pltpu.CompilerParams(vmem_limit_bytes=60 * 1024 * 1024),
    )(tr, th, ssh_new, atm)
    return tr, th, ssh_new.reshape(cells), atm


def solution(mesh):
    placed = (
        P(None, "lev", ("groups", "cells", "sub")),
        P("lev", ("groups", "cells", "sub")),
        P(("groups", "cells", "sub")),
        P(("groups", "cells", "sub")),
        P(None, ("cells", "sub")),
        P(None, ("cells", "sub")),
        P(None, ("cells", "sub")),
        P(("cells", "sub")),
        P(("cells", "sub"), None),
        P(("cells", "sub")),
        P(("cells", "sub")),
    )
    return jax.shard_map(
        functools.partial(per_device, mesh.shape["cells"], mesh.shape["sub"]),
        mesh=mesh,
        in_specs=placed,
        out_specs=(
            P(None, "lev", ("groups", "cells", "sub")),
            P("lev", ("groups", "cells", "sub")),
            P(("groups", "cells", "sub")),
            P(None, ("groups", "cells", "sub")),
        ),
        check_vma=False,
    )
```
